256 devices in a mesh: ctx: 16 (over x_hi, z), head: 16 (over x_lo, y, core).
Axes of the slice: x: 4 (x_hi: 2, x_lo: 2; x = x_hi * 2 + x_lo), y: 4, z: 8, core: 2. Of those that a mesh axis runs over, the one named last changes fastest.
Arguments:
- hidden_in: bfloat16 [2048, 4096], P('ctx'), may hold values from -30 to 30
- query_weight: bfloat16 [4096, 8192], P(None, 'head'), may hold values from -0.1875 to 0.1875
- shared_weight: bfloat16 [4096, 512], P(None, 'head'), may hold values from -0.09375 to 0.09375
- out_weight: bfloat16 [8192, 4096], P('head'), may hold values from -1 to 1
- residual: bfloat16 [2048, 4096], P(('ctx', 'head')), may hold values from -20 to 20
- norm_gain: float32 [4096], replicated, may hold values from 0.25 to 1.75
Outputs:
- residual_out: bfloat16 [2048, 4096], P(('ctx', 'head'))
- normed: bfloat16 [2048, 4096], P('ctx')
The draws below stay inside these ranges and needn't reach their ends.
All inputs are finite; a program needn't handle non-finite values.
Results may differ from the reference program's by a relative error of at most 0.0065.
The reference program's roundings to bfloat16 on the way (of `queries`, `shared`, `mixed` and `attention`) count: a program that leaves them out, or rounds other values in their place, can miss the bound.
Values may be sent and summed in bfloat16 or wider, within the bound.
A program may use at most 64 MiB of HBM per device.

```python
import jax
import jax.numpy as jnp
from jax import lax

D = 4096
HEADS = 64
HD = 128
W1 = 512
W2 = 32
TOK_DEV = 128
TOKENS = 2048


def draw_hidden_in(key, part):
    noise = jnp.clip(jax.random.normal(jax.random.fold_in(key, 11), (TOKENS, D), jnp.float32), -6.0, 6.0)
    return noise.astype(jnp.bfloat16)


def draw_residual(key, part):
    noise = jax.random.normal(jax.random.fold_in(key, 21), (TOKENS, D), jnp.float32)
    return (0.5 * jnp.clip(noise, -6.0, 6.0)).astype(jnp.bfloat16)


def steps_of(own_key, extent, split, least, high):
    gain, own = 1.0, jax.random.fold_in(own_key, 6)
    for dim, blocks in split:
        draws = jnp.exp(jax.random.uniform(jax.random.fold_in(own, dim), (blocks,), jnp.float32, least / len(split), high / len(split)))
        gain = gain * jnp.repeat(draws, extent[dim] // blocks).reshape([-1 if axis == dim else 1 for axis in range(len(extent))])
    return gain


def bell_draw(rng, dims, scale, most, pieces=(), kind=jnp.bfloat16):
    values = scale * jax.random.normal(rng, dims, jnp.float32)
    if pieces:
        values = values * steps_of(rng, dims, pieces, -0.22, 0.18)
    return jnp.clip(values, -most, most).astype(kind)


def setup_inputs(seed: int = 0) -> dict:
    splits = jax.random.split(jax.random.key(seed), 7)
    hidden_in = draw_hidden_in(jax.random.fold_in(splits[6], 71), 0)
    query_weight = bell_draw(splits[1], (D, HEADS * HD), (D // 4) ** -0.5, 0.1875, ((1, 16),))
    shared_weight = bell_draw(splits[2], (D, 4 * HD), D ** -0.5, 0.09375, ((1, 16),))
    out_weight = bell_draw(splits[3], (HEADS * HD, D), (HEADS * HD // 256) ** -0.5, 1.0, ((0, 16),))
    residual = draw_residual(jax.random.fold_in(splits[6], 71), 0)
    norm_gain = jnp.clip(1.0 + 0.15 * jax.random.normal(splits[5], (D,), jnp.float32), 0.25, 1.75)
    return dict(hidden_in=hidden_in, query_weight=query_weight, shared_weight=shared_weight, out_weight=out_weight, residual=residual, norm_gain=norm_gain)


def window_mask(first, rows, spread, reach):
    query_pos = first + jnp.arange(rows, dtype=jnp.int32)[:, None, None]
    offset = jnp.arange(spread, dtype=jnp.int32)[None, :, None]
    column = jnp.arange(rows + reach, dtype=jnp.int32)[None, None, :]
    key_pos = first - reach + column
    allowed = (key_pos <= query_pos) & (key_pos > query_pos - reach) & (key_pos >= 0) & (query_pos - offset >= 0)
    return allowed

def attend_block(query, key_one, value_one, key_two, value_two, valid):
    rows = query.shape[0]
    width = query.shape[1]
    spread = key_two.shape[1]
    mixed = (query[:, None, :].astype(jnp.float32) * key_two.astype(jnp.float32)).astype(jnp.bfloat16)
    scores = jnp.dot(mixed.reshape(rows * spread, width), key_one.T, preferred_element_type=jnp.float32)
    scores = scores.reshape(rows, spread, -1) * width ** (-0.5)
    scores = jnp.where(valid, scores, -jnp.inf)
    peak = lax.optimization_barrier(jnp.max(scores, axis=(1, 2), keepdims=True))
    weights = jnp.exp(scores - peak)
    total = lax.optimization_barrier(jnp.sum(weights, axis=(1, 2)))
    blended = jnp.dot(weights.astype(jnp.bfloat16).reshape(rows * spread, -1), value_one, preferred_element_type=jnp.float32)
    blended = blended.reshape(rows, spread, width)
    return lax.optimization_barrier(jnp.sum(value_two.astype(jnp.float32) * blended, axis=1)) / total[:, None]

def reference(hidden_in, query_weight, shared_weight, out_weight, residual, norm_gain):
    queries = jnp.dot(hidden_in, query_weight, preferred_element_type=jnp.float32).astype(jnp.bfloat16)
    shared = jnp.dot(hidden_in, shared_weight, preferred_element_type=jnp.float32).astype(jnp.bfloat16)
    front_one = jnp.zeros((W1, 2 * HD), jnp.bfloat16)
    front_two = jnp.zeros((W2, 2 * HD), jnp.bfloat16)
    padded_one = jnp.concatenate([front_one, shared[:, :2 * HD]], 0)
    padded_two = jnp.concatenate([front_two, shared[:, 2 * HD:]], 0)
    block = min(128, TOK_DEV)
    heads_q = queries.reshape(TOKENS, HEADS, HD)

    def one_block(number):
        first = (number * block).astype(jnp.int32)
        window = lax.dynamic_slice_in_dim(padded_one, first, block + W1, 0)
        key_one = window[:, :HD]
        value_one = window[:, HD:]
        near = jnp.stack([lax.dynamic_slice_in_dim(padded_two, first + W2 - offset, block, 0) for offset in range(W2)], 1)
        key_two = near[:, :, :HD]
        value_two = near[:, :, HD:]
        valid = window_mask(first, block, W2, W1)
        rows_q = lax.dynamic_slice_in_dim(heads_q, first, block, 0).transpose(1, 0, 2)
        return lax.map(lambda head: attend_block(head, key_one, value_one, key_two, value_two, valid), rows_q)
    outputs = lax.map(one_block, jnp.arange(TOKENS // block, dtype=jnp.int32))
    attention = outputs.transpose(0, 2, 1, 3).reshape(TOKENS, HEADS * HD).astype(jnp.bfloat16)
    projected = jnp.dot(attention, out_weight, preferred_element_type=jnp.float32)
    residual_out = (residual.astype(jnp.float32) + projected).astype(jnp.bfloat16)
    values = residual_out.astype(jnp.float32)
    scale = lax.rsqrt(lax.optimization_barrier(jnp.mean(values * values, axis=1, keepdims=True)) + 1e-05)
    normed = (values * scale * norm_gain).astype(jnp.bfloat16)
    return (residual_out, normed)
```

```python
import functools
import math

import jax
import jax.numpy as jnp
from jax import lax
from jax.experimental import pallas as pl
from jax.experimental.pallas import tpu as pltpu
from jax.sharding import PartitionSpec as P

HD = 128
W1 = 512
W2 = 32
TB = 16
T = 32
REACH = 4
MESH = pl.DeviceIdType.MESH
SCALE = HD**-0.5 * math.log2(math.e)


def kernel(
    hidden_hbm, qw_hbm, sw_hbm, ow_hbm, residual_hbm, gain_hbm,
    rout_ref, normed_hbm,
    hidden, qw, sw, ow, residual, gain,
    kv1, kv2, keys, values, k2e, k2s, v2s, qs, att, sa, sb,
    psib, pown, r1, r2s, r2, ro, nrm,
    load_sem, qw_sem, out_sem,
    a_send, a1_recv, a2_recv, b_send, b1_recv, b2_recv, c_send, c1_recv, c2_recv,
    r1_send, r1_recv, r2_send, r2_recv, ag_send, ag_recv, sh_send, sh_recv,
):
    n_ctx = lax.axis_size("ctx")
    ctx = lax.axis_index("ctx")
    head = lax.axis_index("head")
    core = lax.rem(head, 2)
    chip = head // 2
    y = lax.rem(chip, 4)
    x_lo = chip // 4
    slot = pl.multiple_of(lax.rem(head, 8) * 32, 32)
    tokens, width = hidden_hbm.shape
    heads = qw_hbm.shape[1] // HD
    n_blocks = tokens // T
    steps = tokens // TB
    chunk = width // 16
    sibling = chip * 2 + 1 - core

    def load(src, dst, sem):
        return pltpu.make_async_copy(src, dst, sem)

    parts = 4
    deep = width // parts
    loads = [
        load(hidden_hbm, hidden, load_sem.at[0]),
        load(sw_hbm, sw, load_sem.at[1]),
        load(residual_hbm, residual, load_sem.at[2]),
        load(gain_hbm, gain, load_sem.at[3]),
        load(ow_hbm, ow, load_sem.at[4]),
    ]
    qw_loads = [
        load(qw_hbm.at[pl.ds(k * deep, deep)], qw.at[pl.ds(k * deep, deep)], qw_sem.at[k])
        for k in range(parts)
    ]
    loads[0].start()
    loads[1].start()
    for item in qw_loads:
        item.start()
    for item in loads[2:]:
        item.start()

    def push(src, dst, send, recv, to):
        return pltpu.make_async_remote_copy(
            src_ref=src, dst_ref=dst, send_sem=send, recv_sem=recv, device_id=to, device_id_type=MESH
        )

    barrier = pltpu.get_barrier_semaphore()
    for d in range(1, REACH + 1):
        for xt in range(2):
            pl.semaphore_signal(
                barrier, inc=1, device_id=(lax.rem(ctx + n_ctx - d, n_ctx), xt * 8 + lax.rem(head, 8)),
                device_id_type=MESH,
            )
    for k in range(1, 8):
        pl.semaphore_signal(
            barrier, inc=1, device_id=(ctx, lax.rem(chip + k, 8) * 2 + core), device_id_type=MESH
        )
    pl.semaphore_signal(barrier, inc=1, device_id=(ctx, sibling), device_id_type=MESH)

    loads[0].wait()
    loads[1].wait()
    part = jnp.dot(hidden[...], sw[...], preferred_element_type=jnp.float32)
    part = part.astype(jnp.bfloat16).astype(jnp.float32)
    part = jnp.concatenate([part, jnp.zeros((tokens, HD - 32), jnp.float32)], axis=1)
    part = part.T[:32].astype(jnp.bfloat16)

    mine = pl.ds(slot, 32)

    @pl.when(x_lo == 0)
    def _():
        kv1[0, mine, :] = part

    @pl.when(x_lo == 1)
    def _():
        kv2[0, mine, :] = part

    pl.semaphore_wait(barrier, 2 * REACH + 8)

    def a_copy(buf, recv, d, xt):
        return push(
            buf.at[0, mine], buf.at[d, mine], a_send.at[d, xt], recv.at[d],
            (lax.rem(ctx + d, n_ctx), xt * 8 + lax.rem(head, 8)),
        )

    first_sends = [(0, 1)] + [(d, xt) for d in range(1, REACH + 1) for xt in range(2)]
    second_sends = [(0, 0)] + [(1, xt) for xt in range(2)]

    @pl.when(x_lo == 0)
    def _():
        for d, xt in first_sends:
            a_copy(kv1, a1_recv, d, xt).start()

    @pl.when(x_lo == 1)
    def _():
        for d, xt in second_sends:
            a_copy(kv2, a2_recv, d, xt).start()

    def project(ks):
        total = None
        for k in ks:
            qw_loads[k].wait()
            term = jnp.dot(
                hidden[:, k * deep : (k + 1) * deep], qw[k * deep : (k + 1) * deep, :],
                preferred_element_type=jnp.float32,
            )
            total = term if total is None else total + term
        return total

    half = project((0, 1))
    sa[0:tokens, 0 : heads * HD] = half

    for d in range(1, REACH + 1):
        a_copy(kv1, a1_recv, d, 0).wait_recv()
    a_copy(kv2, a2_recv, 1, 0).wait_recv()

    @pl.when(x_lo == 1)
    def _():
        a_copy(kv1, a1_recv, 0, 0).wait_recv()

    @pl.when(x_lo == 0)
    def _():
        a_copy(kv2, a2_recv, 0, 0).wait_recv()

    def b_copy(which, k):
        buf, recv = ((kv1, b1_recv), (kv2, b2_recv))[which]
        return push(
            buf.at[:, mine], buf.at[:, mine], b_send.at[which, k], recv.at[k],
            (ctx, x_lo * 8 + lax.rem(y + k, 4) * 2 + core),
        )

    def c_copy(which, k):
        buf, recv = ((kv1, c1_recv), (kv2, c2_recv))[which]
        rows = pl.ds(pl.multiple_of((lax.rem(y + 4 - k, 4) * 2 + core) * 32, 32), 32)
        return push(buf.at[:, rows], buf.at[:, rows], c_send.at[which, k], recv.at[k], (ctx, sibling))

    for k in (1, 3, 2):
        for which in (1, 0):
            b_copy(which, k).start()
    for which in (1, 0):
        c_copy(which, 0).start()

    qs[...] = (sa[0:tokens, 0 : heads * HD] + project((2, 3))).astype(jnp.bfloat16)

    for k in (1, 3, 2):
        for which in (1, 0):
            b_copy(which, k).wait_recv()
            c_copy(which, k).start()
    for k in (0, 1, 3, 2):
        c_copy(1, k).wait_recv()

    t_iota = lax.broadcasted_iota(jnp.int32, (tokens, HD), 0)
    for which, dst in ((0, k2s), (1, v2s)):
        rows = slice(which * HD, (which + 1) * HD)
        k2e[0:W2] = kv2[1, rows, :].astype(jnp.float32).T[tokens - W2 :]
        k2e[W2 : W2 + tokens] = kv2[0, rows, :].astype(jnp.float32).T
        for r in range(W2):
            moved = k2e[W2 - r : W2 - r + tokens]
            if r:
                other = k2e[W2 : W2 + tokens] if which == 0 else jnp.zeros_like(moved)
                moved = jnp.where((ctx > 0) | (t_iota >= r), moved, other)
            dst[r] = moved.astype(jnp.bfloat16)

    for k in (0, 1, 3, 2):
        c_copy(0, k).wait_recv()

    own_key = kv1[0, 0:HD, :].astype(jnp.float32) * SCALE
    for d in range(REACH + 1):
        cols = slice((REACH - d) * HD, (REACH - d + 1) * HD)
        key = kv1[d, 0:HD, :].astype(jnp.float32) * SCALE
        value = kv1[d, HD : 2 * HD, :].astype(jnp.float32).T
        ones = jnp.ones((HD, HD), jnp.float32)
        if d:
            here = ctx >= d
            key = jnp.where(here, key, own_key[:, 0:1])
            value = jnp.where(here, value, 0.0)
            ones = jnp.where(here, ones, 0.0)
        high = key.astype(jnp.bfloat16)
        keys[0:HD, cols] = high
        keys[HD : 2 * HD, cols] = (key - high.astype(jnp.float32)).astype(jnp.bfloat16)
        values[cols, 0:HD] = value.astype(jnp.bfloat16)
        values[cols, HD : 2 * HD] = ones.astype(jnp.bfloat16)

    for item in loads[2:]:
        item.wait()

    def scores(h, t0):
        q = qs[pl.ds(t0, TB), h * HD : (h + 1) * HD]
        mixed = (k2s[:, pl.ds(t0, TB), :] * q[None]).reshape(W2 * TB, HD)
        mixed = jnp.concatenate([mixed, mixed], axis=1)
        return jnp.dot(mixed, keys[...], preferred_element_type=jnp.float32)

    def attend(buf, h, t0):
        n = W2 * TB
        s = buf[...].reshape(W2, TB, 5 * HD)
        tok = t0 + lax.broadcasted_iota(jnp.int32, (TB, HD), 0)
        col = lax.broadcasted_iota(jnp.int32, (TB, HD), 1)
        new = (col <= tok)[None]
        both = jnp.where(new, s[:, :, 512:], s[:, :, :128])
        peak = jnp.maximum(
            jnp.maximum(both, s[:, :, 128:256]), jnp.maximum(s[:, :, 256:384], s[:, :, 384:512])
        )
        peak = jnp.max(jnp.max(peak, axis=0), axis=1, keepdims=True)[None]
        shared_w = jnp.exp2(both - peak).astype(jnp.bfloat16).reshape(n, HD)
        newb = jnp.broadcast_to(new, (W2, TB, HD)).reshape(n, HD)
        w_old = jnp.where(newb, 0, shared_w)
        w_new = jnp.where(newb, shared_w, 0)
        w_mid = jnp.exp2(s[:, :, 128:512] - peak).astype(jnp.bfloat16).reshape(n, 3 * HD)
        w = jnp.concatenate([w_old, w_mid, w_new], axis=1)
        o = jnp.dot(w, values[...], preferred_element_type=jnp.float32).reshape(W2, TB, 2 * HD)
        num = jnp.sum(o[:, :, :HD] * v2s[:, pl.ds(t0, TB), :].astype(jnp.float32), axis=0)
        missing = jnp.where(ctx > 0, 0, jnp.maximum(W2 - 1 - tok, 0)).astype(jnp.float32)
        den = jnp.sum(o[:, :, HD:], axis=0) - missing * o[0, :, HD:]
        att[pl.ds(t0, TB), h * HD : (h + 1) * HD] = (num / den).astype(jnp.bfloat16)

    bufs = (sa, sb)
    sa[...] = scores(0, 0)

    def r1_copy(b):
        return push(psib.at[b], r1.at[b], r1_send.at[b], r1_recv.at[b], (ctx, sibling))

    def r2_copy(b, k):
        to = lax.rem(chip + k, 8)
        return push(
            r2s.at[b, to], r2.at[b, k - 1], r2_send.at[b, k - 1], r2_recv.at[b, k - 1], (ctx, to * 2 + core)
        )

    def rows_of(b):
        return pl.ds(pl.multiple_of(b * T, T), T)

    def ag_copy(b, k):
        to = lax.rem(chip + k, 8)
        piece = ro.at[core, chip, rows_of(b)]
        return push(piece, piece, ag_send.at[b, k - 1], ag_recv.at[b, k - 1], (ctx, to * 2 + core))

    def sh_copy(b):
        piece = ro.at[core, :, rows_of(b)]
        return push(piece, piece, sh_send.at[b], sh_recv.at[b], (ctx, sibling))

    def out_copy(b):
        return pltpu.make_async_copy(nrm.at[rows_of(b)], normed_hbm.at[rows_of(b)], out_sem.at[b])

    def product(b, to, to_core):
        cols = pl.ds(pl.multiple_of((to * 2 + to_core) * chunk, chunk), chunk)
        p = jnp.dot(att[rows_of(b), :], ow[:, cols], preferred_element_type=jnp.float32)
        row = lax.broadcasted_iota(jnp.int32, (T, chunk), 0) + (b * T - 8 * head)
        res = residual[:, cols].astype(jnp.float32)
        return p + jnp.where((row >= 0) & (row < 8), jnp.concatenate([res] * (T // 8), axis=0), 0.0)

    def event_project(b):
        def for_sibling(to, _):
            psib[b, to] = product(b, to, 1 - core).astype(jnp.bfloat16)
            return 0

        lax.fori_loop(0, 8, for_sibling, 0)
        r1_copy(b).start()

        def for_self(to, _):
            pown[b, to] = product(b, to, core)
            return 0

        lax.fori_loop(0, 8, for_self, 0)

    def event_scatter(b):
        r1_copy(b).wait_recv()
        for k in (6, 2, 5, 3, 7, 1, 4):
            to = lax.rem(chip + k, 8)
            r2s[b, to] = (pown[b, to] + r1[b, to].astype(jnp.float32)).astype(jnp.bfloat16)
            r2_copy(b, k).start()

    def event_reduce(b):
        total = pown[b, chip] + r1[b, chip].astype(jnp.float32)
        for k in range(1, 8):
            r2_copy(b, k).wait_recv()
        for k in range(1, 8):
            total = total + r2[b, k - 1].astype(jnp.float32)
        ro[core, chip, rows_of(b), :] = total.astype(jnp.bfloat16)
        for k in (6, 2, 5, 3, 7, 1, 4):
            ag_copy(b, k).start()

    def event_share(b):
        for k in range(1, 8):
            to = lax.rem(chip + 8 - k, 8)
            piece = ro.at[core, to, rows_of(b)]
            push(piece, piece, ag_send.at[b, k - 1], ag_recv.at[b, k - 1], (ctx, to * 2 + core)).wait_recv()
        sh_copy(b).start()

    def event_norm(b):
        piece = ro.at[1 - core, :, rows_of(b)]
        push(piece, piece, sh_send.at[b], sh_recv.at[b], (ctx, sibling)).wait_recv()
        square = jnp.zeros((T, chunk), jnp.float32)
        for c in range(2):
            for to in range(8):
                v = ro[c, to, rows_of(b), :].astype(jnp.float32)
                square = square + v * v
        scale = lax.rsqrt(jnp.sum(square, axis=1, keepdims=True) * (1.0 / width) + 1e-05)
        for c in range(2):
            for to in range(8):
                cols = slice((to * 2 + c) * chunk, (to * 2 + c + 1) * chunk)
                v = ro[c, to, rows_of(b), :].astype(jnp.float32)
                nrm[rows_of(b), cols] = (v * scale * gain[:, cols]).astype(jnp.bfloat16)
        out_copy(b).start()

    per = T // TB

    def step(i, _):
        @pl.when(i < steps)
        def _():
            t0 = pl.multiple_of(i * TB, TB)
            later = pl.multiple_of(jnp.minimum(i + 1, steps - 1) * TB, TB)
            for h in range(heads):
                nxt = bufs[(h + 1) % 2]
                if h + 1 < heads:
                    nxt[...] = scores(h + 1, t0)
                else:
                    nxt[...] = scores(0, later)
                attend(bufs[h % 2], h, t0)

        def at(lag, event):
            j = i + 1 - lag
            b = j // per

            @pl.when((j >= per) & (lax.rem(j, per) == 0) & (b <= n_blocks))
            def _():
                event(b - 1)

        at(4, event_norm)
        at(3, event_share)
        at(2, event_reduce)
        at(1, event_scatter)
        at(0, event_project)
        return 0

    lax.fori_loop(0, steps + 4, step, 0)

    for c in range(2):
        for to in range(8):
            cols = slice((to * 2 + c) * chunk, (to * 2 + c + 1) * chunk)
            v = ro[c, to, pl.ds(pl.multiple_of(head // 2 * 16, 16), 16), :].astype(jnp.float32)
            rout_ref[:, cols] = jnp.where(lax.rem(head, 2) == 0, v[:8], v[8:]).astype(jnp.bfloat16)

    @pl.when(x_lo == 0)
    def _():
        for d, xt in first_sends:
            a_copy(kv1, a1_recv, d, xt).wait_send()

    @pl.when(x_lo == 1)
    def _():
        for d, xt in second_sends:
            a_copy(kv2, a2_recv, d, xt).wait_send()

    for which in range(2):
        for k in range(1, 4):
            b_copy(which, k).wait_send()
        for k in range(4):
            c_copy(which, k).wait_send()

    def finish(b, _):
        r1_copy(b).wait_send()
        for k in range(1, 8):
            r2_copy(b, k).wait_send()
            ag_copy(b, k).wait_send()
        sh_copy(b).wait_send()
        out_copy(b).wait()
        return 0

    lax.fori_loop(0, n_blocks, finish, 0)


def body(hidden_in, query_weight, shared_weight, out_weight, residual, norm_gain):
    tokens, width = hidden_in.shape
    columns = query_weight.shape[1]
    blocks = tokens // T
    chunk = width // 16
    vmem = lambda shape, dtype=jnp.bfloat16: pltpu.VMEM(shape, dtype)
    dma = lambda *shape: pltpu.SemaphoreType.DMA(shape)
    anywhere = pl.BlockSpec(memory_space=pl.ANY)
    rows = W2 * TB
    rout, normed = pl.pallas_call(
        kernel,
        out_shape=(
            jax.ShapeDtypeStruct(residual.shape, jnp.bfloat16),
            jax.ShapeDtypeStruct(hidden_in.shape, jnp.bfloat16),
        ),
        in_specs=[anywhere] * 6,
        out_specs=(pl.BlockSpec(memory_space=pltpu.VMEM), anywhere),
        scratch_shapes=[
            vmem((tokens, width)),
            vmem((width, columns)),
            vmem(shared_weight.shape),
            vmem(out_weight.shape),
            vmem(residual.shape),
            vmem((1, width), jnp.float32),
            vmem((REACH + 1, 2 * HD, tokens)),
            vmem((2, 2 * HD, tokens)),
            vmem((2 * HD, (REACH + 1) * HD)),
            vmem(((REACH + 1) * HD, 2 * HD)),
            vmem((W2 + tokens, HD), jnp.float32),
            vmem((W2, tokens, HD)),
            vmem((W2, tokens, HD)),
            vmem((tokens, columns)),
            vmem((tokens, columns)),
            vmem((rows, (REACH + 1) * HD), jnp.float32),
            vmem((rows, (REACH + 1) * HD), jnp.float32),
            vmem((blocks, 8, T, chunk)),
            vmem((blocks, 8, T, chunk), jnp.float32),
            vmem((blocks, 8, T, chunk)),
            vmem((blocks, 8, T, chunk)),
            vmem((blocks, 7, T, chunk)),
            vmem((2, 8, tokens, chunk)),
            vmem((tokens, width)),
            dma(5), dma(4), dma(blocks),
            dma(REACH + 1, 2), dma(REACH + 1), dma(2),
            dma(2, 4), dma(4), dma(4),
            dma(2, 4), dma(4), dma(4),
            dma(blocks), dma(blocks),
            dma(blocks, 7), dma(blocks, 7),
            dma(blocks, 7), dma(blocks, 7),
            dma(blocks), dma(blocks),
        ],
        compiler_params=pltpu.CompilerParams(
            collective_id=0, has_side_effects=True, vmem_limit_bytes=56 * 2**20
        ),
    )(hidden_in, query_weight, shared_weight, out_weight, residual, norm_gain.reshape(1, width))
    return rout, normed


def solution(mesh):
    in_specs = (
        P("ctx", None),
        P(None, "head"),
        P(None, "head"),
        P("head", None),
        P(("ctx", "head"), None),
        P(),
    )
    out_specs = (P(("ctx", "head"), None), P("ctx", None))
    return jax.shard_map(body, mesh=mesh, in_specs=in_specs, out_specs=out_specs, check_vma=False)
```

```python
import functools
import math

import jax
import jax.numpy as jnp
from jax import lax
from jax.experimental import pallas as pl
from jax.experimental.pallas import tpu as pltpu
from jax.sharding import PartitionSpec as P

HD = 128
W1 = 512
W2 = 32
TB = 16
T = 32
REACH = 4
LAGS = (1, 4, 7, 8)
MESH = pl.DeviceIdType.MESH
SCALE = HD**-0.5 * math.log2(math.e)


def kernel(
    hidden_hbm, qw_hbm, sw_hbm, ow_hbm, residual_hbm,
    ro_hbm,
    hidden, qw, sw, ow, residual,
    kv, keys, keys_new, values, values_last, k2e, k2s, v2s, qs, att, sa, na, sb, nb,
    psib, pown, r1, r2s, r2, ro,
    load_sem, qw_sem, out_sem,
    a_send, a_recv, b_send, b_recv, c_send, c_recv,
    r1_send, r1_recv, r2_send, r2_recv, ag_send, ag_recv, sh_send, sh_recv,
):
    n_ctx = lax.axis_size("ctx")
    ctx = lax.axis_index("ctx")
    head = lax.axis_index("head")
    core = lax.rem(head, 2)
    chip = head // 2
    y = lax.rem(chip, 4)
    x_lo = chip // 4
    tokens, width = hidden_hbm.shape
    heads = qw_hbm.shape[1] // HD
    n_blocks = tokens // T
    steps = tokens // TB
    chunk = width // 16
    sibling = chip * 2 + 1 - core

    def load(src, dst, sem):
        return pltpu.make_async_copy(src, dst, sem)

    parts = 4
    deep = width // parts
    loads = [
        load(hidden_hbm, hidden, load_sem.at[0]),
        load(sw_hbm, sw, load_sem.at[1]),
        load(residual_hbm, residual, load_sem.at[2]),
        load(ow_hbm, ow, load_sem.at[3]),
    ]
    qw_loads = [
        load(qw_hbm.at[pl.ds(k * deep, deep)], qw.at[pl.ds(k * deep, deep)], qw_sem.at[k])
        for k in range(parts)
    ]
    loads[0].start()
    loads[1].start()

    def push(src, dst, send, recv, to):
        return pltpu.make_async_remote_copy(
            src_ref=src, dst_ref=dst, send_sem=send, recv_sem=recv, device_id=to, device_id_type=MESH
        )

    barrier = pltpu.get_barrier_semaphore()
    for d in range(1, REACH + 1):
        for xt in range(2):
            pl.semaphore_signal(
                barrier, inc=1, device_id=(lax.rem(ctx + n_ctx - d, n_ctx), xt * 8 + lax.rem(head, 8)),
                device_id_type=MESH,
            )
    for k in range(1, 8):
        pl.semaphore_signal(
            barrier, inc=1, device_id=(ctx, lax.rem(chip + k, 8) * 2 + core), device_id_type=MESH
        )
    pl.semaphore_signal(barrier, inc=1, device_id=(ctx, sibling), device_id_type=MESH)

    loads[0].wait()
    loads[1].wait()
    for item in qw_loads:
        item.start()
    for item in loads[2:]:
        item.start()
    part = lax.dot_general(
        hidden[...], sw[...], (((1,), (1,)), ((), ())), preferred_element_type=jnp.float32
    )
    part = part.astype(jnp.bfloat16).astype(jnp.float32)
    part = jnp.concatenate([part, jnp.zeros((tokens, HD - 32), jnp.float32)], axis=1)
    part = part.T[:32].astype(jnp.bfloat16)

    @pl.when(x_lo == 0)
    def _():
        kv[0, y, core] = part

    @pl.when(x_lo == 1)
    def _():
        kv[1, y, core] = part

    pl.semaphore_wait(barrier, 2 * REACH + 8)

    def a_copy(src, dst, d, xt):
        return push(
            kv.at[src, y, core], kv.at[dst, y, core], a_send.at[dst, xt], a_recv.at[dst],
            (lax.rem(ctx + d, n_ctx), xt * 8 + lax.rem(head, 8)),
        )

    first_sends = [(0, 0, 0, 1)] + [(0, 2 + d, d, xt) for d in (4, 3, 1, 2) for xt in range(2)]
    second_sends = [(1, 1, 0, 0)] + [(1, 2, 1, xt) for xt in range(2)]

    @pl.when(x_lo == 0)
    def _():
        for args in first_sends:
            a_copy(*args).start()

    @pl.when(x_lo == 1)
    def _():
        for args in second_sends:
            a_copy(*args).start()

    def project(ks):
        total = None
        for k in ks:
            qw_loads[k].wait()
            term = jnp.dot(
                hidden[:, k * deep : (k + 1) * deep], qw[k * deep : (k + 1) * deep, :],
                preferred_element_type=jnp.float32,
            )
            total = term if total is None else total + term
        return total

    groups = (slice(0, 2), slice(2, 5), slice(5, 7))

    def b_copy(g, k):
        piece = kv.at[groups[g], y, core]
        return push(
            piece, piece, b_send.at[g], b_recv.at[g],
            (ctx, x_lo * 8 + lax.rem(y + k, 4) * 2 + core),
        )

    def c_copy(g):
        piece = kv.at[groups[g], :, core]
        return push(piece, piece, c_send.at[g], c_recv.at[g], (ctx, sibling))

    def b_all(g):
        piece = kv.at[groups[g], 0:3, core]
        return push(piece, piece, b_send.at[g], b_recv.at[g], (ctx, sibling))

    def spread(g):
        for k in (2, 1, 3):
            b_copy(g, k).start()

    def forward(g):
        b_all(g).wait_recv()
        c_copy(g).start()

    def second(place, which):
        return kv[place, 2 * which : 2 * which + 2].astype(jnp.float32).reshape(HD, tokens)

    sa[0, 0:tokens, 0 : heads * HD] = project((0,))

    @pl.when(x_lo == 1)
    def _():
        a_copy(0, 0, 0, 0).wait_recv()

    @pl.when(x_lo == 0)
    def _():
        a_copy(0, 1, 0, 0).wait_recv()

    spread(0)
    sa[0, 0:tokens, 0 : heads * HD] = sa[0, 0:tokens, 0 : heads * HD] + project((1,))
    for place in (2, 3, 4):
        a_copy(0, place, 0, 0).wait_recv()
    spread(1)
    for place in (5, 6):
        a_copy(0, place, 0, 0).wait_recv()
    spread(2)
    forward(0)
    qs[...] = (sa[0, 0:tokens, 0 : heads * HD] + project((2, 3))).astype(jnp.bfloat16)
    forward(1)
    forward(2)
    c_copy(0).wait_recv()
    c_copy(1).wait_recv()

    t_iota = lax.broadcasted_iota(jnp.int32, (tokens, HD), 0)
    for which, dst in ((0, k2s), (1, v2s)):
        k2e[0:W2] = second(2, which).T[tokens - W2 :]
        k2e[W2 : W2 + tokens] = second(1, which).T
        for r in range(W2):
            moved = k2e[W2 - r : W2 - r + tokens]
            if r:
                other = k2e[W2 : W2 + tokens] if which == 0 else jnp.zeros_like(moved)
                moved = jnp.where((ctx > 0) | (t_iota >= r), moved, other)
            dst[r] = moved.astype(jnp.bfloat16)

    own_key = second(0, 0)
    blank = jnp.zeros((HD, HD), jnp.bfloat16)

    def pair_up(dst, block):
        dst[0:HD, 0:HD] = block
        dst[0:HD, HD : 2 * HD] = blank
        dst[HD : 2 * HD, 0:HD] = blank
        dst[HD : 2 * HD, HD : 2 * HD] = block

    for d in range(REACH + 1):
        if d == 3:
            c_copy(2).wait_recv()
        place = d + 2 if d else 0
        key = second(place, 0)
        value = second(place, 1).T
        ones = jnp.ones((HD, HD), jnp.float32)
        if d:
            here = ctx >= d
            key = jnp.where(here, key, own_key[:, 0:1]) * SCALE
            value = jnp.where(here, value, 0.0)
            ones = jnp.where(here, ones, 0.0)
            cols = slice((REACH - d) * HD, (REACH - d + 1) * HD)
            high = key.astype(jnp.bfloat16)
            keys[0:HD, cols] = high
            keys[HD : 2 * HD, cols] = (key - high.astype(jnp.float32)).astype(jnp.bfloat16)
        else:
            pair_up(keys_new, key.astype(jnp.bfloat16))
        if d == 1:
            pair_up(values_last, value.astype(jnp.bfloat16))
        else:
            first = {4: 0, 0: 1, 3: 2, 2: 3}[d] * HD
            values[first : first + HD, 0:HD] = value.astype(jnp.bfloat16)
            values[first : first + HD, HD : 2 * HD] = ones.astype(jnp.bfloat16)

    for item in loads[2:]:
        item.wait()

    n = W2 * TB

    def scores(pair, t0, buf, buf_new):
        k2 = k2s[:, pl.ds(t0, TB), :]
        mixed = []
        for j in range(2):
            h = pair * 2 + j
            q = qs[pl.ds(t0, TB), h * HD : (h + 1) * HD]
            mixed.append((k2 * q[None]).reshape(n, HD))
        for j in range(2):
            buf[j] = jnp.dot(
                jnp.concatenate([mixed[j], mixed[j]], axis=1), keys[...], preferred_element_type=jnp.float32
            )
        buf_new[...] = jnp.dot(
            jnp.concatenate(mixed, axis=1), keys_new[...], preferred_element_type=jnp.float32
        )

    def attend(pair, t0, buf, buf_new):
        tok = t0 + lax.broadcasted_iota(jnp.int32, (TB, HD), 0)
        col = lax.broadcasted_iota(jnp.int32, (TB, HD), 1)
        new = (col <= tok)[None]
        new_rows = jnp.broadcast_to(new, (W2, TB, HD)).reshape(n, HD)
        outs, last, last_sums = [], [], []
        for j in range(2):
            s = buf[j].reshape(W2, TB, 4 * HD)
            s_new = buf_new[:, j * HD : (j + 1) * HD].reshape(W2, TB, HD) * SCALE
            both = jnp.where(new, s_new, s[:, :, :HD])
            peak = jnp.maximum(
                jnp.maximum(both, s[:, :, HD : 2 * HD]),
                jnp.maximum(s[:, :, 2 * HD : 3 * HD], s[:, :, 3 * HD :]),
            )
            peak = jnp.max(jnp.max(peak, axis=0), axis=1, keepdims=True)[None]
            w_both = jnp.exp2(both - peak).astype(jnp.bfloat16).reshape(n, HD)
            w_old = jnp.where(new_rows, 0, w_both)
            w_new = jnp.where(new_rows, w_both, 0)
            w_mid = jnp.exp2(s[:, :, HD : 3 * HD] - peak).astype(jnp.bfloat16).reshape(n, 2 * HD)
            w_last = jnp.exp2(s[:, :, 3 * HD :] - peak)
            last_sums.append(jnp.sum(jnp.sum(w_last, axis=0), axis=1, keepdims=True))
            last.append(w_last.astype(jnp.bfloat16).reshape(n, HD))
            outs.append(
                jnp.dot(
                    jnp.concatenate([w_old, w_new, w_mid], axis=1), values[...],
                    preferred_element_type=jnp.float32,
                )
            )
        out_last = jnp.dot(
            jnp.concatenate(last, axis=1), values_last[...], preferred_element_type=jnp.float32
        )
        v2 = v2s[:, pl.ds(t0, TB), :].astype(jnp.float32)
        missing = jnp.where(ctx > 0, 0, jnp.maximum(W2 - 1 - tok, 0)).astype(jnp.float32)
        for j in range(2):
            h = pair * 2 + j
            o = outs[j].reshape(W2, TB, 2 * HD)
            o_last = out_last[:, j * HD : (j + 1) * HD].reshape(W2, TB, HD)
            num = jnp.sum((o[:, :, :HD] + o_last) * v2, axis=0)
            den = jnp.sum(o[:, :, HD:], axis=0) - missing * o[0, :, HD:]
            den = den + jnp.where(ctx > 0, last_sums[j], 0.0)
            att[pl.ds(t0, TB), h * HD : (h + 1) * HD] = (num / den).astype(jnp.bfloat16)

    scores(0, 0, sa, na)

    def r1_copy(b):
        return push(psib.at[b], r1.at[b], r1_send.at[b], r1_recv.at[b], (ctx, sibling))

    def r2_copy(b, k):
        to = lax.rem(chip + k, 8)
        return push(
            r2s.at[b, to], r2.at[b, k - 1], r2_send.at[b], r2_recv.at[b], (ctx, to * 2 + core)
        )

    def rows_of(b):
        return pl.ds(pl.multiple_of(b * T, T), T)

    def ag_copy(b, k):
        to = lax.rem(chip + k, 8)
        piece = ro.at[core, chip, rows_of(b)]
        return push(piece, piece, ag_send.at[b], ag_recv.at[b], (ctx, to * 2 + core))

    def r2_all(b):
        return push(r2s.at[b, 0:7], r2.at[b], r2_send.at[b], r2_recv.at[b], (ctx, sibling))

    def ag_all(b):
        pieces = ro.at[core, 0:7, rows_of(b)]
        return push(pieces, pieces, ag_send.at[b], ag_recv.at[b], (ctx, sibling))

    def sh_copy(b):
        piece = ro.at[core, :, rows_of(b)]
        return push(piece, piece, sh_send.at[b], sh_recv.at[b], (ctx, sibling))

    def out_copy(b):
        return pltpu.make_async_copy(ro.at[:, :, rows_of(b)], ro_hbm.at[:, :, rows_of(b)], out_sem.at[b])

    def product(b, to, to_core):
        cols = pl.ds(pl.multiple_of((to * 2 + to_core) * chunk, chunk), chunk)
        p = jnp.dot(att[rows_of(b), :], ow[:, cols], preferred_element_type=jnp.float32)
        row = lax.broadcasted_iota(jnp.int32, (T, chunk), 0) + (b * T - 8 * head)
        res = residual[:, cols].astype(jnp.float32)
        return p + jnp.where((row >= 0) & (row < 8), jnp.concatenate([res] * (T // 8), axis=0), 0.0)

    def event_project(b):
        for to in range(8):
            psib[b, to] = product(b, to, 1 - core).astype(jnp.bfloat16)
        r1_copy(b).start()
        for to in range(8):
            pown[b, to] = product(b, to, core)

    def event_scatter(b):
        r1_copy(b).wait_recv()
        for k in (6, 2, 5, 3, 7, 1, 4):
            to = lax.rem(chip + k, 8)
            r2s[b, to] = (pown[b, to] + r1[b, to].astype(jnp.float32)).astype(jnp.bfloat16)
            r2_copy(b, k).start()

    def event_reduce(b):
        total = pown[b, chip] + r1[b, chip].astype(jnp.float32)
        r2_all(b).wait_recv()
        for k in range(1, 8):
            total = total + r2[b, k - 1].astype(jnp.float32)
        ro[core, chip, rows_of(b), :] = total.astype(jnp.bfloat16)
        for k in (6, 2, 5, 3, 7, 1, 4):
            ag_copy(b, k).start()

    def event_share(b):
        ag_all(b).wait_recv()
        sh_copy(b).start()

    def event_leave(b):
        piece = ro.at[1 - core, :, rows_of(b)]
        push(piece, piece, sh_send.at[b], sh_recv.at[b], (ctx, sibling)).wait_recv()
        out_copy(b).start()

    per = T // TB

    def finish(b, _):
        r1_copy(b).wait_send()
        r2_all(b).wait_send()
        ag_all(b).wait_send()
        sh_copy(b).wait_send()
        out_copy(b).wait()
        return 0

    def settle():
        @pl.when(x_lo == 0)
        def _():
            for args in first_sends:
                a_copy(*args).wait_send()

        @pl.when(x_lo == 1)
        def _():
            for args in second_sends:
                a_copy(*args).wait_send()

        for g in range(3):
            b_all(g).wait_send()
            c_copy(g).wait_send()

    def step(i, _):
        @pl.when(i < steps)
        def _():
            t0 = pl.multiple_of(i * TB, TB)
            later = pl.multiple_of(jnp.minimum(i + 1, steps - 1) * TB, TB)
            scores(1, t0, sb, nb)
            attend(0, t0, sa, na)
            scores(0, later, sa, na)
            attend(1, t0, sb, nb)

        def at(lag, event):
            j = i + 1 - lag
            b = j // per

            @pl.when((j >= per) & (lax.rem(j, per) == 0) & (b <= n_blocks))
            def _():
                event(b - 1)

        @pl.when(i == steps + LAGS[0])
        def _():
            settle()

        at(LAGS[3], event_leave)
        at(LAGS[2], event_share)
        at(LAGS[1], event_reduce)
        at(LAGS[0], event_scatter)
        at(0, event_project)
        return 0

    lax.fori_loop(0, steps + LAGS[3], step, 0)

    lax.fori_loop(0, n_blocks, finish, 0)


def norm_kernel(ro, gain, rout_ref, normed_ref):
    head = lax.axis_index("head")
    tokens, width = normed_ref.shape
    chunk = width // 16
    square = jnp.zeros((tokens, chunk), jnp.float32)
    for c in range(2):
        for to in range(8):
            v = ro[c, to].astype(jnp.float32)
            square = square + v * v
    scale = lax.rsqrt(jnp.sum(square, axis=1, keepdims=True) * (1.0 / width) + 1e-05)
    for c in range(2):
        for to in range(8):
            cols = slice((to * 2 + c) * chunk, (to * 2 + c + 1) * chunk)
            normed_ref[:, cols] = (ro[c, to].astype(jnp.float32) * scale * gain[:, cols]).astype(jnp.bfloat16)
            v = ro[c, to, pl.ds(pl.multiple_of(head // 2 * 16, 16), 16), :].astype(jnp.float32)
            rout_ref[:, cols] = jnp.where(lax.rem(head, 2) == 0, v[:8], v[8:]).astype(jnp.bfloat16)


def body(hidden_in, query_weight, shared_weight, out_weight, residual, norm_gain):
    tokens, width = hidden_in.shape
    columns = query_weight.shape[1]
    blocks = tokens // T
    chunk = width // 16
    vmem = lambda shape, dtype=jnp.bfloat16: pltpu.VMEM(shape, dtype)
    dma = lambda *shape: pltpu.SemaphoreType.DMA(shape)
    anywhere = pl.BlockSpec(memory_space=pl.ANY)
    rows = W2 * TB
    whole = pl.BlockSpec(memory_space=pltpu.VMEM)
    gathered = pl.pallas_call(
        kernel,
        out_shape=jax.ShapeDtypeStruct((2, 8, tokens, chunk), jnp.bfloat16),
        in_specs=[anywhere] * 5,
        out_specs=anywhere,
        scratch_shapes=[
            vmem((tokens, width)),
            vmem((width, columns)),
            vmem(shared_weight.shape[::-1]),
            vmem(out_weight.shape),
            vmem(residual.shape),
            vmem((REACH + 3, 4, 2, 32, tokens)),
            vmem((2 * HD, REACH * HD)),
            vmem((2 * HD, 2 * HD)),
            vmem((REACH * HD, 2 * HD)),
            vmem((2 * HD, 2 * HD)),
            vmem((W2 + tokens, HD), jnp.float32),
            vmem((W2, tokens, HD)),
            vmem((W2, tokens, HD)),
            vmem((tokens, columns)),
            vmem((tokens, columns)),
            vmem((2, rows, REACH * HD), jnp.float32),
            vmem((rows, 2 * HD), jnp.float32),
            vmem((2, rows, REACH * HD), jnp.float32),
            vmem((rows, 2 * HD), jnp.float32),
            vmem((blocks, 8, T, chunk)),
            vmem((blocks, 8, T, chunk), jnp.float32),
            vmem((blocks, 8, T, chunk)),
            vmem((blocks, 8, T, chunk)),
            vmem((blocks, 7, T, chunk)),
            vmem((2, 8, tokens, chunk)),
            dma(4), dma(4), dma(blocks),
            dma(REACH + 3, 2), dma(REACH + 3),
            dma(3), dma(3),
            dma(3), dma(3),
            dma(blocks), dma(blocks),
            dma(blocks), dma(blocks),
            dma(blocks), dma(blocks),
            dma(blocks), dma(blocks),
        ],
        compiler_params=pltpu.CompilerParams(
            collective_id=0, has_side_effects=True, vmem_limit_bytes=56 * 2**20
        ),
    )(hidden_in, query_weight, shared_weight.T, out_weight, residual)
    return tuple(
        pl.pallas_call(
            norm_kernel,
            out_shape=(
                jax.ShapeDtypeStruct(residual.shape, jnp.bfloat16),
                jax.ShapeDtypeStruct(hidden_in.shape, jnp.bfloat16),
            ),
            in_specs=[whole] * 2,
            out_specs=(whole, whole),
        )(gathered, norm_gain.reshape(1, width))
    )


def solution(mesh):
    in_specs = (
        P("ctx", None),
        P(None, "head"),
        P(None, "head"),
        P("head", None),
        P(("ctx", "head"), None),
        P(),
    )
    out_specs = (P(("ctx", "head"), None), P("ctx", None))
    return jax.shard_map(body, mesh=mesh, in_specs=in_specs, out_specs=out_specs, check_vma=False)
```

```python
import functools
import math

import jax
import jax.numpy as jnp
from jax import lax
from jax.experimental import pallas as pl
from jax.experimental.pallas import tpu as pltpu
from jax.sharding import PartitionSpec as P

HD = 128
W1 = 512
W2 = 32
TB = 16
T = 32
REACH = 4
LAGS = (1, 4, 7, 8)
MESH = pl.DeviceIdType.MESH
SCALE = HD**-0.5 * math.log2(math.e)


def kernel(
    hidden_hbm, qw_hbm, sw_hbm, ow_hbm, residual_hbm,
    ro_hbm,
    hidden, qw, sw, ow, residual,
    kv, keys, keys_new, values, values_last, k2e, k2s, v2s, qs, att, sa, na, sb, nb,
    psib, pown, r1, r2s, r2, ro,
    load_sem, qw_sem, out_sem,
    a_send, a_recv, b_send, b_recv, c_send, c_recv,
    r1_send, r1_recv, r2_send, r2_recv, ag_send, ag_recv, sh_send, sh_recv,
):
    n_ctx = lax.axis_size("ctx")
    ctx = lax.axis_index("ctx")
    head = lax.axis_index("head")
    core = lax.rem(head, 2)
    chip = head // 2
    y = lax.rem(chip, 4)
    x_lo = chip // 4
    tokens, width = hidden_hbm.shape
    heads = qw_hbm.shape[1] // HD
    n_blocks = tokens // T
    steps = tokens // TB
    chunk = width // 16
    sibling = chip * 2 + 1 - core

    def load(src, dst, sem):
        return pltpu.make_async_copy(src, dst, sem)

    parts = 4
    deep = width // parts
    loads = [
        load(hidden_hbm, hidden, load_sem.at[0]),
        load(sw_hbm, sw, load_sem.at[1]),
        load(residual_hbm, residual, load_sem.at[2]),
        load(ow_hbm, ow, load_sem.at[3]),
    ]
    qw_loads = [
        load(qw_hbm.at[pl.ds(k * deep, deep)], qw.at[pl.ds(k * deep, deep)], qw_sem.at[k])
        for k in range(parts)
    ]
    loads[0].start()
    loads[1].start()

    def push(src, dst, send, recv, to):
        return pltpu.make_async_remote_copy(
            src_ref=src, dst_ref=dst, send_sem=send, recv_sem=recv, device_id=to, device_id_type=MESH
        )

    barrier = pltpu.get_barrier_semaphore()
    for d in range(1, REACH + 1):
        for xt in range(2):
            pl.semaphore_signal(
                barrier, inc=1, device_id=(lax.rem(ctx + n_ctx - d, n_ctx), xt * 8 + lax.rem(head, 8)),
                device_id_type=MESH,
            )
    for k in range(1, 8):
        pl.semaphore_signal(
            barrier, inc=1, device_id=(ctx, lax.rem(chip + k, 8) * 2 + core), device_id_type=MESH
        )
    pl.semaphore_signal(barrier, inc=1, device_id=(ctx, sibling), device_id_type=MESH)

    loads[0].wait()
    loads[1].wait()
    for item in qw_loads:
        item.start()
    for item in loads[2:]:
        item.start()
    part = lax.dot_general(
        hidden[...], sw[...], (((1,), (1,)), ((), ())), preferred_element_type=jnp.float32
    )
    part = part.astype(jnp.bfloat16).astype(jnp.float32)
    part = jnp.concatenate([part, jnp.zeros((tokens, HD - 32), jnp.float32)], axis=1)
    part = part.T[:32].astype(jnp.bfloat16)

    @pl.when(x_lo == 0)
    def _():
        kv[0, y, core] = part

    @pl.when(x_lo == 1)
    def _():
        kv[1, y, core] = part

    pl.semaphore_wait(barrier, 2 * REACH + 8)

    def a_copy(src, dst, d, xt):
        return push(
            kv.at[src, y, core], kv.at[dst, y, core], a_send.at[dst, xt], a_recv.at[dst],
            (lax.rem(ctx + d, n_ctx), xt * 8 + lax.rem(head, 8)),
        )

    first_sends = [(0, 2 + d, d, xt) for d in (4, 3) for xt in range(2)] + [(0, 0, 0, 1)]
    first_sends += [(0, 2 + d, d, xt) for d in (1, 2) for xt in range(2)]
    second_sends = [(1, 1, 0, 0)] + [(1, 2, 1, xt) for xt in range(2)]

    @pl.when(x_lo == 0)
    def _():
        for args in first_sends:
            a_copy(*args).start()

    @pl.when(x_lo == 1)
    def _():
        for args in second_sends:
            a_copy(*args).start()

    def project(ks):
        total = None
        for k in ks:
            qw_loads[k].wait()
            term = jnp.dot(
                hidden[:, k * deep : (k + 1) * deep], qw[k * deep : (k + 1) * deep, :],
                preferred_element_type=jnp.float32,
            )
            total = term if total is None else total + term
        return total

    groups = (slice(0, 4), slice(4, 7))

    def b_copy(g, k):
        piece = kv.at[groups[g], y, core]
        return push(
            piece, piece, b_send.at[g], b_recv.at[g],
            (ctx, x_lo * 8 + lax.rem(y + k, 4) * 2 + core),
        )

    def c_copy(g):
        piece = kv.at[groups[g], :, core]
        return push(piece, piece, c_send.at[g], c_recv.at[g], (ctx, sibling))

    def b_all(g):
        piece = kv.at[groups[g], 0:3, core]
        return push(piece, piece, b_send.at[g], b_recv.at[g], (ctx, sibling))

    def spread(g):
        for k in (2, 1, 3):
            b_copy(g, k).start()

    def forward(g):
        b_all(g).wait_recv()
        c_copy(g).start()

    def second(place, which):
        return kv[place, 2 * which : 2 * which + 2].astype(jnp.float32).reshape(HD, tokens)

    sa[0, 0:tokens, 0 : heads * HD] = project((0, 1))

    @pl.when(x_lo == 1)
    def _():
        a_copy(0, 0, 0, 0).wait_recv()

    @pl.when(x_lo == 0)
    def _():
        a_copy(0, 1, 0, 0).wait_recv()

    for place in (2, 3):
        a_copy(0, place, 0, 0).wait_recv()
    spread(0)
    qs[...] = (sa[0, 0:tokens, 0 : heads * HD] + project((2, 3))).astype(jnp.bfloat16)
    for place in (4, 5, 6):
        a_copy(0, place, 0, 0).wait_recv()
    spread(1)
    forward(0)
    c_copy(0).wait_recv()

    t_iota = lax.broadcasted_iota(jnp.int32, (tokens, HD), 0)
    for which, dst in ((0, k2s), (1, v2s)):
        k2e[0:W2] = second(2, which).T[tokens - W2 :]
        k2e[W2 : W2 + tokens] = second(1, which).T
        for r in range(W2):
            moved = k2e[W2 - r : W2 - r + tokens]
            if r:
                other = k2e[W2 : W2 + tokens] if which == 0 else jnp.zeros_like(moved)
                moved = jnp.where((ctx > 0) | (t_iota >= r), moved, other)
            dst[r] = moved.astype(jnp.bfloat16)

    forward(1)

    own_key = second(0, 0)
    blank = jnp.zeros((HD, HD), jnp.bfloat16)

    def pair_up(dst, block):
        dst[0:HD, 0:HD] = block
        dst[0:HD, HD : 2 * HD] = blank
        dst[HD : 2 * HD, 0:HD] = blank
        dst[HD : 2 * HD, HD : 2 * HD] = block

    for d in range(REACH + 1):
        if d == 2:
            c_copy(1).wait_recv()
        place = d + 2 if d else 0
        key = second(place, 0)
        value = second(place, 1).T
        ones = jnp.ones((HD, HD), jnp.float32)
        if d:
            here = ctx >= d
            key = jnp.where(here, key, own_key[:, 0:1]) * SCALE
            value = jnp.where(here, value, 0.0)
            ones = jnp.where(here, ones, 0.0)
            cols = slice((REACH - d) * HD, (REACH - d + 1) * HD)
            high = key.astype(jnp.bfloat16)
            keys[0:HD, cols] = high
            keys[HD : 2 * HD, cols] = (key - high.astype(jnp.float32)).astype(jnp.bfloat16)
        else:
            pair_up(keys_new, key.astype(jnp.bfloat16))
        if d == 1:
            pair_up(values_last, value.astype(jnp.bfloat16))
        else:
            first = {4: 0, 0: 1, 3: 2, 2: 3}[d] * HD
            values[first : first + HD, 0:HD] = value.astype(jnp.bfloat16)
            values[first : first + HD, HD : 2 * HD] = ones.astype(jnp.bfloat16)

    for item in loads[2:]:
        item.wait()

    n = W2 * TB

    def scores(pair, t0, buf, buf_new):
        k2 = k2s[:, pl.ds(t0, TB), :]
        mixed = []
        for j in range(2):
            h = pair * 2 + j
            q = qs[pl.ds(t0, TB), h * HD : (h + 1) * HD]
            mixed.append((k2 * q[None]).reshape(n, HD))
        for j in range(2):
            buf[j] = jnp.dot(
                jnp.concatenate([mixed[j], mixed[j]], axis=1), keys[...], preferred_element_type=jnp.float32
            )
        buf_new[...] = jnp.dot(
            jnp.concatenate(mixed, axis=1), keys_new[...], preferred_element_type=jnp.float32
        )

    def attend(pair, t0, buf, buf_new):
        tok = t0 + lax.broadcasted_iota(jnp.int32, (TB, HD), 0)
        col = lax.broadcasted_iota(jnp.int32, (TB, HD), 1)
        new = (col <= tok)[None]
        new_rows = jnp.broadcast_to(new, (W2, TB, HD)).reshape(n, HD)
        outs, last, last_sums = [], [], []
        for j in range(2):
            s = buf[j].reshape(W2, TB, 4 * HD)
            s_new = buf_new[:, j * HD : (j + 1) * HD].reshape(W2, TB, HD) * SCALE
            both = jnp.where(new, s_new, s[:, :, :HD])
            peak = jnp.maximum(
                jnp.maximum(both, s[:, :, HD : 2 * HD]),
                jnp.maximum(s[:, :, 2 * HD : 3 * HD], s[:, :, 3 * HD :]),
            )
            peak = jnp.max(jnp.max(peak, axis=0), axis=1, keepdims=True)[None]
            w_both = jnp.exp2(both - peak).astype(jnp.bfloat16).reshape(n, HD)
            w_old = jnp.where(new_rows, 0, w_both)
            w_new = jnp.where(new_rows, w_both, 0)
            w_mid = jnp.exp2(s[:, :, HD : 3 * HD] - peak).astype(jnp.bfloat16).reshape(n, 2 * HD)
            w_last = jnp.exp2(s[:, :, 3 * HD :] - peak)
            last_sums.append(jnp.sum(jnp.sum(w_last, axis=0), axis=1, keepdims=True))
            last.append(w_last.astype(jnp.bfloat16).reshape(n, HD))
            outs.append(
                jnp.dot(
                    jnp.concatenate([w_old, w_new, w_mid], axis=1), values[...],
                    preferred_element_type=jnp.float32,
                )
            )
        out_last = jnp.dot(
            jnp.concatenate(last, axis=1), values_last[...], preferred_element_type=jnp.float32
        )
        v2 = v2s[:, pl.ds(t0, TB), :].astype(jnp.float32)
        missing = jnp.where(ctx > 0, 0, jnp.maximum(W2 - 1 - tok, 0)).astype(jnp.float32)
        for j in range(2):
            h = pair * 2 + j
            o = outs[j].reshape(W2, TB, 2 * HD)
            o_last = out_last[:, j * HD : (j + 1) * HD].reshape(W2, TB, HD)
            num = jnp.sum((o[:, :, :HD] + o_last) * v2, axis=0)
            den = jnp.sum(o[:, :, HD:], axis=0) - missing * o[0, :, HD:]
            den = den + jnp.where(ctx > 0, last_sums[j], 0.0)
            att[pl.ds(t0, TB), h * HD : (h + 1) * HD] = (num / den).astype(jnp.bfloat16)

    scores(0, 0, sa, na)

    def other(k):
        return lax.rem(x_lo + k // 4, 2) * 4 + lax.rem(y + k % 4, 4)

    def r1_copy(b):
        return push(psib.at[b], r1.at[b], r1_send.at[b], r1_recv.at[b], (ctx, sibling))

    def r2_copy(b, k):
        to = other(k)
        return push(
            r2s.at[b, to], r2.at[b, k - 1], r2_send.at[b], r2_recv.at[b], (ctx, to * 2 + core)
        )

    def rows_of(b):
        return pl.ds(pl.multiple_of(b * T, T), T)

    def ag_copy(b, k):
        to = other(k)
        piece = ro.at[core, chip, rows_of(b)]
        return push(piece, piece, ag_send.at[b], ag_recv.at[b], (ctx, to * 2 + core))

    def r2_all(b):
        return push(r2s.at[b, 0:7], r2.at[b], r2_send.at[b], r2_recv.at[b], (ctx, sibling))

    def ag_all(b):
        pieces = ro.at[core, 0:7, rows_of(b)]
        return push(pieces, pieces, ag_send.at[b], ag_recv.at[b], (ctx, sibling))

    def sh_copy(b):
        piece = ro.at[core, :, rows_of(b)]
        return push(piece, piece, sh_send.at[b], sh_recv.at[b], (ctx, sibling))

    def out_copy(b):
        return pltpu.make_async_copy(ro.at[:, :, rows_of(b)], ro_hbm.at[:, :, rows_of(b)], out_sem.at[b])

    def product(b, to, to_core):
        cols = pl.ds(pl.multiple_of((to * 2 + to_core) * chunk, chunk), chunk)
        p = jnp.dot(att[rows_of(b), :], ow[:, cols], preferred_element_type=jnp.float32)
        row = lax.broadcasted_iota(jnp.int32, (T, chunk), 0) + (b * T - 8 * head)
        res = residual[:, cols].astype(jnp.float32)
        return p + jnp.where((row >= 0) & (row < 8), jnp.concatenate([res] * (T // 8), axis=0), 0.0)

    def event_project(b):
        for to in range(8):
            psib[b, to] = product(b, to, 1 - core).astype(jnp.bfloat16)
        r1_copy(b).start()
        for to in range(8):
            pown[b, to] = product(b, to, core)

    def event_scatter(b):
        r1_copy(b).wait_recv()
        for k in (6, 2, 5, 7, 1, 3, 4):
            to = other(k)
            r2s[b, to] = (pown[b, to] + r1[b, to].astype(jnp.float32)).astype(jnp.bfloat16)
            r2_copy(b, k).start()

    def event_reduce(b):
        total = pown[b, chip] + r1[b, chip].astype(jnp.float32)
        r2_all(b).wait_recv()
        for k in range(1, 8):
            total = total + r2[b, k - 1].astype(jnp.float32)
        ro[core, chip, rows_of(b), :] = total.astype(jnp.bfloat16)
        for k in (6, 2, 5, 7, 1, 3, 4):
            ag_copy(b, k).start()

    def event_share(b):
        ag_all(b).wait_recv()
        sh_copy(b).start()

    def event_leave(b):
        piece = ro.at[1 - core, :, rows_of(b)]
        push(piece, piece, sh_send.at[b], sh_recv.at[b], (ctx, sibling)).wait_recv()
        out_copy(b).start()

    per = T // TB

    def finish(b, _):
        r1_copy(b).wait_send()
        r2_all(b).wait_send()
        ag_all(b).wait_send()
        sh_copy(b).wait_send()
        out_copy(b).wait()
        return 0

    def settle():
        @pl.when(x_lo == 0)
        def _():
            for args in first_sends:
                a_copy(*args).wait_send()

        @pl.when(x_lo == 1)
        def _():
            for args in second_sends:
                a_copy(*args).wait_send()

        for g in range(2):
            b_all(g).wait_send()
            c_copy(g).wait_send()

    def step(i, _):
        @pl.when(i < steps)
        def _():
            t0 = pl.multiple_of(i * TB, TB)
            later = pl.multiple_of(jnp.minimum(i + 1, steps - 1) * TB, TB)
            scores(1, t0, sb, nb)
            attend(0, t0, sa, na)
            scores(0, later, sa, na)
            attend(1, t0, sb, nb)

        def at(lag, event):
            j = i + 1 - lag
            b = j // per

            @pl.when((j >= per) & (lax.rem(j, per) == 0) & (b <= n_blocks))
            def _():
                event(b - 1)

        @pl.when(i == steps + LAGS[0])
        def _():
            settle()

        at(LAGS[3], event_leave)
        at(LAGS[2], event_share)
        at(LAGS[1], event_reduce)
        at(LAGS[0], event_scatter)
        at(0, event_project)
        return 0

    lax.fori_loop(0, steps + LAGS[3], step, 0)

    lax.fori_loop(0, n_blocks, finish, 0)


def norm_kernel(ro, gain, rout_ref, normed_ref):
    head = lax.axis_index("head")
    some, width = normed_ref.shape
    chunk = width // 16
    square = jnp.zeros((some, chunk), jnp.float32)
    for c in range(2):
        for to in range(8):
            v = ro[c, to].astype(jnp.float32)
            square = square + v * v
    scale = lax.rsqrt(jnp.sum(square, axis=1, keepdims=True) * (1.0 / width) + 1e-05)
    for c in range(2):
        for to in range(8):
            cols = slice((to * 2 + c) * chunk, (to * 2 + c + 1) * chunk)
            normed_ref[:, cols] = (ro[c, to].astype(jnp.float32) * scale * gain[:, cols]).astype(jnp.bfloat16)

    per = some // 8

    @pl.when(pl.program_id(0) == head // per)
    def _():
        row = pl.multiple_of(lax.rem(head, per) // 2 * 16, 16)
        for c in range(2):
            for to in range(8):
                cols = slice((to * 2 + c) * chunk, (to * 2 + c + 1) * chunk)
                v = ro[c, to, pl.ds(row, 16), :].astype(jnp.float32)
                rout_ref[:, cols] = jnp.where(lax.rem(head, 2) == 0, v[:8], v[8:]).astype(jnp.bfloat16)


def body(hidden_in, query_weight, shared_weight, out_weight, residual, norm_gain):
    tokens, width = hidden_in.shape
    columns = query_weight.shape[1]
    blocks = tokens // T
    chunk = width // 16
    vmem = lambda shape, dtype=jnp.bfloat16: pltpu.VMEM(shape, dtype)
    dma = lambda *shape: pltpu.SemaphoreType.DMA(shape)
    anywhere = pl.BlockSpec(memory_space=pl.ANY)
    rows = W2 * TB
    whole = pl.BlockSpec(memory_space=pltpu.VMEM)
    gathered = pl.pallas_call(
        kernel,
        out_shape=jax.ShapeDtypeStruct((2, 8, tokens, chunk), jnp.bfloat16),
        in_specs=[anywhere] * 5,
        out_specs=anywhere,
        scratch_shapes=[
            vmem((tokens, width)),
            vmem((width, columns)),
            vmem(shared_weight.shape[::-1]),
            vmem(out_weight.shape),
            vmem(residual.shape),
            vmem((REACH + 3, 4, 2, 32, tokens)),
            vmem((2 * HD, REACH * HD)),
            vmem((2 * HD, 2 * HD)),
            vmem((REACH * HD, 2 * HD)),
            vmem((2 * HD, 2 * HD)),
            vmem((W2 + tokens, HD), jnp.float32),
            vmem((W2, tokens, HD)),
            vmem((W2, tokens, HD)),
            vmem((tokens, columns)),
            vmem((tokens, columns)),
            vmem((2, rows, REACH * HD), jnp.float32),
            vmem((rows, 2 * HD), jnp.float32),
            vmem((2, rows, REACH * HD), jnp.float32),
            vmem((rows, 2 * HD), jnp.float32),
            vmem((blocks, 8, T, chunk)),
            vmem((blocks, 8, T, chunk), jnp.float32),
            vmem((blocks, 8, T, chunk)),
            vmem((blocks, 8, T, chunk)),
            vmem((blocks, 7, T, chunk)),
            vmem((2, 8, tokens, chunk)),
            dma(4), dma(4), dma(blocks),
            dma(REACH + 3, 2), dma(REACH + 3),
            dma(2), dma(2),
            dma(2), dma(2),
            dma(blocks), dma(blocks),
            dma(blocks), dma(blocks),
            dma(blocks), dma(blocks),
            dma(blocks), dma(blocks),
        ],
        compiler_params=pltpu.CompilerParams(
            collective_id=0, has_side_effects=True, vmem_limit_bytes=56 * 2**20
        ),
    )(hidden_in, query_weight, shared_weight.T, out_weight, residual)
    return tuple(
        pl.pallas_call(
            norm_kernel,
            out_shape=(
                jax.ShapeDtypeStruct(residual.shape, jnp.bfloat16),
                jax.ShapeDtypeStruct(hidden_in.shape, jnp.bfloat16),
            ),
            grid=(2,),
            in_specs=[
                pl.BlockSpec((2, 8, tokens // 2, chunk), lambda i: (0, 0, i, 0)),
                pl.BlockSpec((1, width), lambda i: (0, 0)),
            ],
            out_specs=(
                pl.BlockSpec(residual.shape, lambda i: (0, 0)),
                pl.BlockSpec((tokens // 2, width), lambda i: (i, 0)),
            ),
        )(gathered, norm_gain.reshape(1, width))
    )


def solution(mesh):
    in_specs = (
        P("ctx", None),
        P(None, "head"),
        P(None, "head"),
        P("head", None),
        P(("ctx", "head"), None),
        P(),
    )
    out_specs = (P(("ctx", "head"), None), P("ctx", None))
    return jax.shard_map(body, mesh=mesh, in_specs=in_specs, out_specs=out_specs, check_vma=False)
```

```python
import functools
import math

import jax
import jax.numpy as jnp
from jax import lax
from jax.experimental import pallas as pl
from jax.experimental.pallas import tpu as pltpu
from jax.sharding import PartitionSpec as P

HD = 128
W1 = 512
W2 = 32
TB = 16
T = 32
REACH = 4
LAGS = (1, 3, 5, 6)
MESH = pl.DeviceIdType.MESH
SCALE = HD**-0.5 * math.log2(math.e)


def kernel(
    hidden_hbm, qw_hbm, sw_hbm, ow_hbm, residual_hbm,
    ro_hbm,
    hidden, qw, sw, ow, residual,
    kv, keys, keys_new, values, values_last, k2e, k2s, v2s, qs, att, sa, na, sb, nb,
    psib, pown, r1, r2s, r2, ro,
    load_sem, qw_sem, out_sem,
    a_send, a_recv, b_send, b_recv, c_send, c_recv,
    r1_send, r1_recv, r2_send, r2_recv, ag_send, ag_recv, sh_send, sh_recv,
):
    n_ctx = lax.axis_size("ctx")
    ctx = lax.axis_index("ctx")
    head = lax.axis_index("head")
    core = lax.rem(head, 2)
    chip = head // 2
    y = lax.rem(chip, 4)
    x_lo = chip // 4
    tokens, width = hidden_hbm.shape
    heads = qw_hbm.shape[1] // HD
    n_blocks = tokens // T
    chunk = width // 16
    sibling = chip * 2 + 1 - core

    def load(src, dst, sem):
        return pltpu.make_async_copy(src, dst, sem)

    parts = 4
    deep = width // parts
    loads = [
        load(hidden_hbm, hidden, load_sem.at[0]),
        load(sw_hbm, sw, load_sem.at[1]),
        load(residual_hbm, residual, load_sem.at[2]),
        load(ow_hbm, ow, load_sem.at[3]),
    ]
    qw_loads = [
        load(qw_hbm.at[pl.ds(k * deep, deep)], qw.at[pl.ds(k * deep, deep)], qw_sem.at[k])
        for k in range(parts)
    ]
    loads[0].start()
    loads[1].start()

    def push(src, dst, send, recv, to):
        return pltpu.make_async_remote_copy(
            src_ref=src, dst_ref=dst, send_sem=send, recv_sem=recv, device_id=to, device_id_type=MESH
        )

    barrier = pltpu.get_barrier_semaphore()
    for d in range(1, REACH + 1):
        for xt in range(2):
            pl.semaphore_signal(
                barrier, inc=1, device_id=(lax.rem(ctx + n_ctx - d, n_ctx), xt * 8 + lax.rem(head, 8)),
                device_id_type=MESH,
            )
    for k in range(1, 8):
        pl.semaphore_signal(
            barrier, inc=1, device_id=(ctx, lax.rem(chip + k, 8) * 2 + core), device_id_type=MESH
        )
    pl.semaphore_signal(barrier, inc=1, device_id=(ctx, sibling), device_id_type=MESH)

    loads[0].wait()
    loads[1].wait()
    for item in qw_loads:
        item.start()
    for item in loads[2:]:
        item.start()
    part = lax.dot_general(
        hidden[...], sw[...], (((1,), (1,)), ((), ())), preferred_element_type=jnp.float32
    )
    part = part.astype(jnp.bfloat16).astype(jnp.float32)
    part = jnp.concatenate([part, jnp.zeros((tokens, HD - 32), jnp.float32)], axis=1)
    part = part.T[:32].astype(jnp.bfloat16)

    @pl.when(x_lo == 0)
    def _():
        kv[0, y, core] = part

    @pl.when(x_lo == 1)
    def _():
        kv[1, y, core] = part

    pl.semaphore_wait(barrier, 2 * REACH + 8)

    def a_copy(src, dst, d, xt):
        return push(
            kv.at[src, y, core], kv.at[dst, y, core], a_send.at[dst, xt], a_recv.at[dst],
            (lax.rem(ctx + d, n_ctx), xt * 8 + lax.rem(head, 8)),
        )

    first_sends = [(0, 2 + d, d, xt) for d in (4, 3) for xt in range(2)] + [(0, 0, 0, 1)]
    first_sends += [(0, 2 + d, d, xt) for d in (1, 2) for xt in range(2)]
    second_sends = [(1, 1, 0, 0)] + [(1, 2, 1, xt) for xt in range(2)]

    @pl.when(x_lo == 0)
    def _():
        for args in first_sends:
            a_copy(*args).start()

    @pl.when(x_lo == 1)
    def _():
        for args in second_sends:
            a_copy(*args).start()

    def project(ks):
        total = None
        for k in ks:
            qw_loads[k].wait()
            term = jnp.dot(
                hidden[:, k * deep : (k + 1) * deep], qw[k * deep : (k + 1) * deep, :],
                preferred_element_type=jnp.float32,
            )
            total = term if total is None else total + term
        return total

    groups = (slice(0, 4), slice(4, 7))

    def b_copy(g, k):
        piece = kv.at[groups[g], y, core]
        return push(
            piece, piece, b_send.at[g], b_recv.at[g],
            (ctx, x_lo * 8 + lax.rem(y + k, 4) * 2 + core),
        )

    def c_copy(g):
        piece = kv.at[groups[g], :, core]
        return push(piece, piece, c_send.at[g], c_recv.at[g], (ctx, sibling))

    def b_all(g):
        piece = kv.at[groups[g], 0:3, core]
        return push(piece, piece, b_send.at[g], b_recv.at[g], (ctx, sibling))

    def spread(g):
        for k in (2, 1, 3):
            b_copy(g, k).start()

    def forward(g):
        b_all(g).wait_recv()
        c_copy(g).start()

    def second(place, which):
        return kv[place, 2 * which : 2 * which + 2].astype(jnp.float32).reshape(HD, tokens)

    sa[0, 0:tokens, 0 : heads * HD] = project((0, 1))

    @pl.when(x_lo == 1)
    def _():
        a_copy(0, 0, 0, 0).wait_recv()

    @pl.when(x_lo == 0)
    def _():
        a_copy(0, 1, 0, 0).wait_recv()

    for place in (2, 3):
        a_copy(0, place, 0, 0).wait_recv()
    spread(0)
    qs[...] = (sa[0, 0:tokens, 0 : heads * HD] + project((2, 3))).astype(jnp.bfloat16)
    for place in (4, 5, 6):
        a_copy(0, place, 0, 0).wait_recv()
    spread(1)
    forward(0)
    c_copy(0).wait_recv()

    t_iota = lax.broadcasted_iota(jnp.int32, (tokens, HD), 0)
    for which, dst in ((0, k2s), (1, v2s)):
        k2e[0:W2] = second(2, which).T[tokens - W2 :]
        k2e[W2 : W2 + tokens] = second(1, which).T
        for r in range(W2):
            moved = k2e[W2 - r : W2 - r + tokens]
            if r:
                other = k2e[W2 : W2 + tokens] if which == 0 else jnp.zeros_like(moved)
                moved = jnp.where((ctx > 0) | (t_iota >= r), moved, other)
            dst[r] = moved.astype(jnp.bfloat16)

    forward(1)

    own_key = second(0, 0)
    blank = jnp.zeros((HD, HD), jnp.bfloat16)

    def pair_up(dst, block):
        dst[0:HD, 0:HD] = block
        dst[0:HD, HD : 2 * HD] = blank
        dst[HD : 2 * HD, 0:HD] = blank
        dst[HD : 2 * HD, HD : 2 * HD] = block

    for d in range(REACH + 1):
        if d == 2:
            c_copy(1).wait_recv()
        place = d + 2 if d else 0
        key = second(place, 0)
        value = second(place, 1).T
        ones = jnp.ones((HD, HD), jnp.float32)
        if d:
            here = ctx >= d
            key = jnp.where(here, key, own_key[:, 0:1]) * SCALE
            value = jnp.where(here, value, 0.0)
            ones = jnp.where(here, ones, 0.0)
            cols = slice((REACH - d) * HD, (REACH - d + 1) * HD)
            high = key.astype(jnp.bfloat16)
            keys[0:HD, cols] = high
            keys[HD : 2 * HD, cols] = (key - high.astype(jnp.float32)).astype(jnp.bfloat16)
        else:
            pair_up(keys_new, key.astype(jnp.bfloat16))
        if d == 1:
            pair_up(values_last, value.astype(jnp.bfloat16))
        else:
            first = {4: 0, 0: 1, 3: 2, 2: 3}[d] * HD
            values[first : first + HD, 0:HD] = value.astype(jnp.bfloat16)
            values[first : first + HD, HD : 2 * HD] = ones.astype(jnp.bfloat16)

    for item in loads[2:]:
        item.wait()

    n = W2 * TB

    def scores(pair, t0, buf, buf_new):
        k2 = k2s[:, pl.ds(t0, TB), :]
        mixed = []
        for j in range(2):
            h = pair * 2 + j
            q = qs[pl.ds(t0, TB), h * HD : (h + 1) * HD]
            mixed.append((k2 * q[None]).reshape(n, HD))
        for j in range(2):
            buf[j] = jnp.dot(
                jnp.concatenate([mixed[j], mixed[j]], axis=1), keys[...], preferred_element_type=jnp.float32
            )
        buf_new[...] = jnp.dot(
            jnp.concatenate(mixed, axis=1), keys_new[...], preferred_element_type=jnp.float32
        )

    def attend(pair, t0, buf, buf_new):
        tok = t0 + lax.broadcasted_iota(jnp.int32, (TB, HD), 0)
        col = lax.broadcasted_iota(jnp.int32, (TB, HD), 1)
        new = (col <= tok)[None]
        new_rows = jnp.broadcast_to(new, (W2, TB, HD)).reshape(n, HD)
        outs, last, last_sums = [], [], []
        for j in range(2):
            s = buf[j].reshape(W2, TB, 4 * HD)
            s_new = buf_new[:, j * HD : (j + 1) * HD].reshape(W2, TB, HD) * SCALE
            both = jnp.where(new, s_new, s[:, :, :HD])
            peak = jnp.maximum(
                jnp.maximum(both, s[:, :, HD : 2 * HD]),
                jnp.maximum(s[:, :, 2 * HD : 3 * HD], s[:, :, 3 * HD :]),
            )
            peak = jnp.max(jnp.max(peak, axis=0), axis=1, keepdims=True)[None]
            w_both = jnp.exp2(both - peak).astype(jnp.bfloat16).reshape(n, HD)
            w_old = jnp.where(new_rows, 0, w_both)
            w_new = jnp.where(new_rows, w_both, 0)
            w_mid = jnp.exp2(s[:, :, HD : 3 * HD] - peak).astype(jnp.bfloat16).reshape(n, 2 * HD)
            w_last = jnp.exp2(s[:, :, 3 * HD :] - peak)
            last_sums.append(jnp.sum(jnp.sum(w_last, axis=0), axis=1, keepdims=True))
            last.append(w_last.astype(jnp.bfloat16).reshape(n, HD))
            outs.append(
                jnp.dot(
                    jnp.concatenate([w_old, w_new, w_mid], axis=1), values[...],
                    preferred_element_type=jnp.float32,
                )
            )
        out_last = jnp.dot(
            jnp.concatenate(last, axis=1), values_last[...], preferred_element_type=jnp.float32
        )
        v2 = v2s[:, pl.ds(t0, TB), :].astype(jnp.float32)
        missing = jnp.where(ctx > 0, 0, jnp.maximum(W2 - 1 - tok, 0)).astype(jnp.float32)
        for j in range(2):
            h = pair * 2 + j
            o = outs[j].reshape(W2, TB, 2 * HD)
            o_last = out_last[:, j * HD : (j + 1) * HD].reshape(W2, TB, HD)
            num = jnp.sum((o[:, :, :HD] + o_last) * v2, axis=0)
            den = jnp.sum(o[:, :, HD:], axis=0) - missing * o[0, :, HD:]
            den = den + jnp.where(ctx > 0, last_sums[j], 0.0)
            att[pl.ds(t0, TB), h * HD : (h + 1) * HD] = (num / den).astype(jnp.bfloat16)

    scores(0, 0, sa, na)

    def other(k):
        return lax.rem(x_lo + k // 4, 2) * 4 + lax.rem(y + k % 4, 4)

    def r1_copy(b):
        return push(psib.at[b], r1.at[b], r1_send.at[b], r1_recv.at[b], (ctx, sibling))

    def r2_copy(b, k):
        to = other(k)
        return push(
            r2s.at[b, to], r2.at[b, k - 1], r2_send.at[b], r2_recv.at[b], (ctx, to * 2 + core)
        )

    def rows_of(b):
        return pl.ds(pl.multiple_of(b * T, T), T)

    def ag_copy(b, k):
        to = other(k)
        piece = ro.at[core, chip, rows_of(b)]
        return push(piece, piece, ag_send.at[b], ag_recv.at[b], (ctx, to * 2 + core))

    def r2_all(b):
        return push(r2s.at[b, 0:7], r2.at[b], r2_send.at[b], r2_recv.at[b], (ctx, sibling))

    def ag_all(b):
        pieces = ro.at[core, 0:7, rows_of(b)]
        return push(pieces, pieces, ag_send.at[b], ag_recv.at[b], (ctx, sibling))

    def sh_copy(b):
        piece = ro.at[core, :, rows_of(b)]
        return push(piece, piece, sh_send.at[b], sh_recv.at[b], (ctx, sibling))

    def out_copy(b):
        return pltpu.make_async_copy(ro.at[:, :, rows_of(b)], ro_hbm.at[:, :, rows_of(b)], out_sem.at[b])

    def product(b, to, to_core):
        cols = pl.ds(pl.multiple_of((to * 2 + to_core) * chunk, chunk), chunk)
        p = jnp.dot(att[rows_of(b), :], ow[:, cols], preferred_element_type=jnp.float32)
        row = lax.broadcasted_iota(jnp.int32, (T, chunk), 0) + (b * T - 8 * head)
        res = residual[:, cols].astype(jnp.float32)
        return p + jnp.where((row >= 0) & (row < 8), jnp.concatenate([res] * (T // 8), axis=0), 0.0)

    def event_project(b):
        for to in range(8):
            psib[b, to] = product(b, to, 1 - core).astype(jnp.bfloat16)
        r1_copy(b).start()
        for to in range(8):
            pown[b, to] = product(b, to, core)

    def event_scatter(b):
        r1_copy(b).wait_recv()
        for k in (6, 2, 5, 7, 1, 3, 4):
            to = other(k)
            r2s[b, to] = (pown[b, to] + r1[b, to].astype(jnp.float32)).astype(jnp.bfloat16)
            r2_copy(b, k).start()

    def event_reduce(b):
        total = pown[b, chip] + r1[b, chip].astype(jnp.float32)
        r2_all(b).wait_recv()
        for k in range(1, 8):
            total = total + r2[b, k - 1].astype(jnp.float32)
        ro[core, chip, rows_of(b), :] = total.astype(jnp.bfloat16)
        for k in (6, 2, 5, 7, 1, 3, 4):
            ag_copy(b, k).start()

    def event_share(b):
        ag_all(b).wait_recv()
        sh_copy(b).start()

    def event_leave(b):
        piece = ro.at[1 - core, :, rows_of(b)]
        push(piece, piece, sh_send.at[b], sh_recv.at[b], (ctx, sibling)).wait_recv()
        out_copy(b).start()

    per = T // TB

    def finish(b, _):
        r1_copy(b).wait_send()
        r2_all(b).wait_send()
        ag_all(b).wait_send()
        sh_copy(b).wait_send()
        out_copy(b).wait()
        return 0

    def settle():
        @pl.when(x_lo == 0)
        def _():
            for args in first_sends:
                a_copy(*args).wait_send()

        @pl.when(x_lo == 1)
        def _():
            for args in second_sends:
                a_copy(*args).wait_send()

        for g in range(2):
            b_all(g).wait_send()
            c_copy(g).wait_send()

    def step(i, _):
        @pl.when(i < n_blocks)
        def _():
            for u in range(per):
                t0 = pl.multiple_of(i * T + u * TB, TB)
                later = pl.multiple_of(jnp.minimum(i * T + (u + 1) * TB, tokens - TB), TB)
                scores(1, t0, sb, nb)
                attend(0, t0, sa, na)
                scores(0, later, sa, na)
                attend(1, t0, sb, nb)

        def at(lag, event):
            @pl.when((i >= lag) & (i - lag < n_blocks))
            def _():
                event(i - lag)

        at(LAGS[0], event_scatter)
        at(0, event_project)
        at(LAGS[1], event_reduce)

        @pl.when(i == n_blocks)
        def _():
            settle()

        at(LAGS[2], event_share)
        at(LAGS[3], event_leave)
        return 0

    lax.fori_loop(0, n_blocks + LAGS[3], step, 0)

    lax.fori_loop(0, n_blocks, finish, 0)


def norm_kernel(ro, gain, rout_ref, normed_ref):
    head = lax.axis_index("head")
    some, width = normed_ref.shape
    chunk = width // 16
    square = jnp.zeros((some, chunk), jnp.float32)
    for c in range(2):
        for to in range(8):
            v = ro[c, to].astype(jnp.float32)
            square = square + v * v
    scale = lax.rsqrt(jnp.sum(square, axis=1, keepdims=True) * (1.0 / width) + 1e-05)
    for c in range(2):
        for to in range(8):
            cols = slice((to * 2 + c) * chunk, (to * 2 + c + 1) * chunk)
            normed_ref[:, cols] = (ro[c, to].astype(jnp.float32) * scale * gain[:, cols]).astype(jnp.bfloat16)

    per = some // 8

    @pl.when(pl.program_id(0) == head // per)
    def _():
        row = pl.multiple_of(lax.rem(head, per) // 2 * 16, 16)
        for c in range(2):
            for to in range(8):
                cols = slice((to * 2 + c) * chunk, (to * 2 + c + 1) * chunk)
                v = ro[c, to, pl.ds(row, 16), :].astype(jnp.float32)
                rout_ref[:, cols] = jnp.where(lax.rem(head, 2) == 0, v[:8], v[8:]).astype(jnp.bfloat16)


def body(hidden_in, query_weight, shared_weight, out_weight, residual, norm_gain):
    tokens, width = hidden_in.shape
    columns = query_weight.shape[1]
    blocks = tokens // T
    chunk = width // 16
    vmem = lambda shape, dtype=jnp.bfloat16: pltpu.VMEM(shape, dtype)
    dma = lambda *shape: pltpu.SemaphoreType.DMA(shape)
    anywhere = pl.BlockSpec(memory_space=pl.ANY)
    rows = W2 * TB
    whole = pl.BlockSpec(memory_space=pltpu.VMEM)
    gathered = pl.pallas_call(
        kernel,
        out_shape=jax.ShapeDtypeStruct((2, 8, tokens, chunk), jnp.bfloat16),
        in_specs=[anywhere] * 5,
        out_specs=anywhere,
        scratch_shapes=[
            vmem((tokens, width)),
            vmem((width, columns)),
            vmem(shared_weight.shape[::-1]),
            vmem(out_weight.shape),
            vmem(residual.shape),
            vmem((REACH + 3, 4, 2, 32, tokens)),
            vmem((2 * HD, REACH * HD)),
            vmem((2 * HD, 2 * HD)),
            vmem((REACH * HD, 2 * HD)),
            vmem((2 * HD, 2 * HD)),
            vmem((W2 + tokens, HD), jnp.float32),
            vmem((W2, tokens, HD)),
            vmem((W2, tokens, HD)),
            vmem((tokens, columns)),
            vmem((tokens, columns)),
            vmem((2, rows, REACH * HD), jnp.float32),
            vmem((rows, 2 * HD), jnp.float32),
            vmem((2, rows, REACH * HD), jnp.float32),
            vmem((rows, 2 * HD), jnp.float32),
            vmem((blocks, 8, T, chunk)),
            vmem((blocks, 8, T, chunk), jnp.float32),
            vmem((blocks, 8, T, chunk)),
            vmem((blocks, 8, T, chunk)),
            vmem((blocks, 7, T, chunk)),
            vmem((2, 8, tokens, chunk)),
            dma(4), dma(4), dma(blocks),
            dma(REACH + 3, 2), dma(REACH + 3),
            dma(2), dma(2),
            dma(2), dma(2),
            dma(blocks), dma(blocks),
            dma(blocks), dma(blocks),
            dma(blocks), dma(blocks),
            dma(blocks), dma(blocks),
        ],
        compiler_params=pltpu.CompilerParams(
            collective_id=0, has_side_effects=True, vmem_limit_bytes=56 * 2**20
        ),
    )(hidden_in, query_weight, shared_weight.T, out_weight, residual)
    return tuple(
        pl.pallas_call(
            norm_kernel,
            out_shape=(
                jax.ShapeDtypeStruct(residual.shape, jnp.bfloat16),
                jax.ShapeDtypeStruct(hidden_in.shape, jnp.bfloat16),
            ),
            grid=(2,),
            in_specs=[
                pl.BlockSpec((2, 8, tokens // 2, chunk), lambda i: (0, 0, i, 0)),
                pl.BlockSpec((1, width), lambda i: (0, 0)),
            ],
            out_specs=(
                pl.BlockSpec(residual.shape, lambda i: (0, 0)),
                pl.BlockSpec((tokens // 2, width), lambda i: (i, 0)),
            ),
        )(gathered, norm_gain.reshape(1, width))
    )


def solution(mesh):
    in_specs = (
        P("ctx", None),
        P(None, "head"),
        P(None, "head"),
        P("head", None),
        P(("ctx", "head"), None),
        P(),
    )
    out_specs = (P(("ctx", "head"), None), P("ctx", None))
    return jax.shard_map(body, mesh=mesh, in_specs=in_specs, out_specs=out_specs, check_vma=False)
```
